512 devices in a mesh: sub: 64 (over z_lo, y, x), grp: 8 (over z_hi, core).
Axes of the slice: x: 4, y: 4, z: 16 (z_hi: 4, z_lo: 4; z = z_hi * 4 + z_lo), core: 2. Of those that a mesh axis runs over, the one named last changes fastest.
Arguments:
- residual: bfloat16 [8, 128, 6, 128, 256], P('grp', 'sub'), may hold values from -6 to 6
- sub_matrix: bfloat16 [8, 128, 12, 3, 128, 128], P('grp', 'sub'), may hold values from -0.15625 to 0.15625
- diag_inverse: bfloat16 [8, 128, 12, 128, 128], P('grp', 'sub'), may hold values from -0.5 to 0.5
- tile_cols: int32 [8, 128, 12, 3], P('grp', 'sub'), may hold values from 0 to 11
- outgoing_rows: int32 [8, 128, 2, 3], P('grp', 'sub'), may hold values from 0 to 5
- coarse_basis: bfloat16 [8, 128, 64, 6, 128], P('grp', 'sub'), may hold values from -0.21875 to 0.21875
- coarse_blocks: float32 [8, 128, 3, 64, 64], P('grp', 'sub'), may hold values from -0.375 to 0.375
- coarse_inverse: float32 [8, 128, 64, 64], P('grp', 'sub'), may hold values from -0.75 to 0.75
- coarse_links: int32 [8, 128, 2], P('grp', 'sub'), may hold values 0 or 1
Outputs:
- preconditioned: bfloat16 [8, 128, 6, 128, 256], P('grp', 'sub')
The draws below stay inside these ranges and needn't reach their ends.
All inputs are finite; a program needn't handle non-finite values. No bound on the sum of `coarse_links` on one device may be relied on, other than what follows from the above.
Results may differ from the reference program's by a relative error of at most 0.0057.
Values may be sent and summed in bfloat16 or wider, within the bound.
A program may use at most 64 MiB of HBM per device.

```python
import jax
import jax.numpy as jnp
from jax import lax

TILE = 128
COARSE_VECTORS = 64
PER_ROW = 3
OVER = 3
SWEEPS = 2
CSWEEPS = 2
OWN = 6
RHS = 256
EXT = 12
GROUPS = 8
SUBDOMAINS = 128


def set_ends(array, key, least, high):
    shape = array.shape
    index_at = [jax.random.randint(jax.random.fold_in(key, axis), (), 0, shape[axis]) for axis in range(len(shape))]
    array = array.at[tuple(index_at)].set(least)
    longest = shape.index(max(shape))
    index_at[longest] = (index_at[longest] + 1) % shape[longest]
    return array.at[tuple(index_at)].set(high)


def level_of(rng, dims, shards, low, top_value):
    def one(dim, shards_of):
        steps = jax.random.uniform(jax.random.fold_in(jax.random.fold_in(rng, 6), dim), (shards_of,), jnp.float32, low / len(shards), top_value / len(shards))
        return jnp.repeat(jnp.exp(steps), dims[dim] // shards_of).reshape((-1,) + (1,) * (len(dims) - dim - 1))

    loudness = one(*shards[0])
    for cut in shards[1:]:
        loudness = loudness * one(*cut)
    return loudness


def normal_values(own_key, dims, scale, most, shards=(), kind=jnp.bfloat16):
    gain = level_of(own_key, dims, shards, -0.22, 0.18) if shards else 1.0
    entries = jax.random.normal(own_key, dims, jnp.float32) * scale * gain
    return jnp.minimum(jnp.maximum(entries, -most), most).astype(kind)


def setup_inputs(seed: int = 0) -> dict:
    key_of = jax.random.split(jax.random.key(seed), 10)
    residual = normal_values(key_of[0], (GROUPS, SUBDOMAINS, OWN, TILE, RHS), 1.0, 6.0, ((0, 8), (1, 64)))
    sub_matrix = normal_values(key_of[1], (GROUPS, SUBDOMAINS, EXT, PER_ROW, TILE, TILE), (4 * PER_ROW * TILE) ** -0.5, 0.15625, ((0, 8), (1, 64)))
    diag_inverse = normal_values(key_of[2], (GROUPS, SUBDOMAINS, EXT, TILE, TILE), TILE ** -0.5, 0.5, ((0, 8), (1, 64)))
    tile_cols = set_ends(jax.random.randint(key_of[3], (GROUPS, SUBDOMAINS, EXT, PER_ROW), 0, EXT), jax.random.fold_in(key_of[3], 1), 0, EXT - 1).astype(jnp.int32)
    outgoing_rows = set_ends(jax.random.randint(key_of[4], (GROUPS, SUBDOMAINS, 2, OVER), 0, OWN), jax.random.fold_in(key_of[4], 1), 0, OWN - 1).astype(jnp.int32)
    coarse_basis = normal_values(key_of[5], (GROUPS, SUBDOMAINS, COARSE_VECTORS, OWN, TILE), (OWN * TILE) ** -0.5, 0.21875, ((0, 8), (1, 64)))
    coarse_blocks = normal_values(key_of[6], (GROUPS, SUBDOMAINS, 3, COARSE_VECTORS, COARSE_VECTORS), (4 * COARSE_VECTORS) ** -0.5, 0.375, ((0, 8), (1, 64)), jnp.float32)
    coarse_inverse = normal_values(key_of[7], (GROUPS, SUBDOMAINS, COARSE_VECTORS, COARSE_VECTORS), COARSE_VECTORS ** -0.5, 0.75, ((0, 8), (1, 64)), jnp.float32)
    coarse_links = set_ends((jax.random.randint(key_of[8], (GROUPS, SUBDOMAINS, 2), 0, 4) < 3).astype(jnp.int32), jax.random.fold_in(key_of[8], 1), 0, 1)
    return dict(residual=residual, sub_matrix=sub_matrix, diag_inverse=diag_inverse, tile_cols=tile_cols, outgoing_rows=outgoing_rows, coarse_basis=coarse_basis, coarse_blocks=coarse_blocks, coarse_inverse=coarse_inverse, coarse_links=coarse_links)


def received_rows(block, rows):
    return jnp.take(block, rows.astype(jnp.int32), axis=0)


def place_rows(rows, entry_values):
    marks = (rows[:, None] == jnp.arange(OWN, dtype=jnp.int32)[None, :]).astype(jnp.float32)
    return jnp.einsum('on,otr->ntr', marks, entry_values.astype(jnp.float32))


def extend_layer(layer_res, layer_rows):
    left = jax.vmap(received_rows)(layer_res[:-1], layer_rows[:-1, 1])
    right = jax.vmap(received_rows)(layer_res[1:], layer_rows[1:, 0])
    zero = jnp.zeros((1, OVER, TILE, RHS), layer_res.dtype)
    left = jnp.concatenate([zero, left], 0)
    right = jnp.concatenate([right, zero], 0)
    return jnp.concatenate([left, layer_res, right], 1)


def local_sweeps(operands):
    b_ext, tiles, inverse, cols = operands
    inverse_f = inverse.astype(jnp.float32)
    b_f = b_ext.astype(jnp.float32)
    x = jnp.einsum('eij,ejr->eir', inverse_f, b_f).astype(jnp.bfloat16)
    for sweep in range(SWEEPS):
        picked = jnp.take(x, cols.astype(jnp.int32), axis=0)
        image = jnp.einsum('ekij,ekjr->eir', tiles.astype(jnp.float32), picked.astype(jnp.float32))
        defect = (b_f - image).astype(jnp.bfloat16)
        x = (x.astype(jnp.float32) + jnp.einsum('eij,ejr->eir', inverse_f, defect.astype(jnp.float32))).astype(jnp.bfloat16)
    return x


def fine_layer(layer_res, layer_mat, layer_inv, layer_cols, layer_rows):
    b_ext = extend_layer(layer_res, layer_rows)
    x = lax.map(local_sweeps, (b_ext, layer_mat, layer_inv, layer_cols))
    own = x[:, OVER:OVER + OWN].astype(jnp.float32)
    from_next = jax.vmap(place_rows)(layer_rows[:-1, 1], x[1:, :OVER])
    from_prev = jax.vmap(place_rows)(layer_rows[1:, 0], x[:-1, OVER + OWN:])
    zero = jnp.zeros((1, OWN, TILE, RHS), jnp.float32)
    return own + jnp.concatenate([from_next, zero], 0) + jnp.concatenate([zero, from_prev], 0)


def coarse_update(right_hand_side, blocks, inverse, links, coarse_level, below, above):
    hi = lax.Precision.HIGHEST
    mult = lambda m, v: jnp.einsum('...ab,...br->...ar', m, v, precision=hi)
    defect = right_hand_side - mult(blocks[..., 0, :, :], coarse_level)
    defect = defect - links[..., 0][..., None, None] * mult(blocks[..., 1, :, :], below)
    defect = defect - links[..., 1][..., None, None] * mult(blocks[..., 2, :, :], above)
    return coarse_level + mult(inverse, defect)


def reference(residual, sub_matrix, diag_inverse, tile_cols, outgoing_rows, coarse_basis, coarse_blocks, coarse_inverse, coarse_links):
    def restrict(operands):
        basis, res = operands
        return jnp.einsum('scnt,sntr->scr', basis.astype(jnp.float32), res.astype(jnp.float32))

    right_hand_side = lax.map(restrict, (coarse_basis, residual))
    links = coarse_links.astype(jnp.float32)
    coarse_level = jnp.einsum('gsab,gsbr->gsar', coarse_inverse, right_hand_side, precision=lax.Precision.HIGHEST)
    for step in range(CSWEEPS):
        zero = jnp.zeros_like(coarse_level[:1])
        below = jnp.concatenate([zero, coarse_level[:-1]], 0)
        above = jnp.concatenate([coarse_level[1:], zero], 0)
        coarse_level = coarse_update(right_hand_side, coarse_blocks, coarse_inverse, links, coarse_level, below, above)
    level_b = coarse_level.astype(jnp.bfloat16)

    def finish(operands):
        res, mat, inv, cols, rows, basis, lev = operands
        fine = fine_layer(res, mat, inv, cols, rows)
        spread = jnp.einsum('scnt,scr->sntr', basis.astype(jnp.float32), lev.astype(jnp.float32))
        return (fine + spread).astype(jnp.bfloat16)

    return lax.map(finish, (residual, sub_matrix, diag_inverse, tile_cols, outgoing_rows, coarse_basis, level_b))
```

```python
import jax
import jax.numpy as jnp
from jax import lax
from jax.experimental import pallas as pl
from jax.experimental.pallas import tpu as pltpu
from jax.sharding import PartitionSpec as P

MESH = pl.DeviceIdType.MESH
BF = jnp.bfloat16
F32 = jnp.float32
OWN, EXT, LEND, TILE, RHS, COARSE = 6, 12, 3, 128, 256, 64
WIDTH = 128
CHUNKS = RHS // WIDTH


def mm(a, b):
    return jnp.dot(a, b, preferred_element_type=F32)


def split(a):
    hi = a.astype(BF)
    return hi, (a - hi.astype(F32)).astype(BF)


def cols_of(c):
    return slice(c * WIDTH, (c + 1) * WIDTH)


def kernel(
    res_h, mat_h, inv_h, cols_h, rows_h, bas_h, blk_h, cinv_h, links_h,
    out,
    cols, rows, links, res, mat, inv, bas, blk, cinv, bast,
    x0f, x0, x1, x2, pre,
    lsend, lrecv, rsend, rrecv,
    qa, ia, xq, lv0, lv, csend, lev_b,
    load_sem, ls_sem, lr_sem, rs_sem, rr_sem, cs_sem, cr_sem,
):
    sub = lax.axis_index("sub")
    grp = lax.axis_index("grp")
    subs = lax.axis_size("sub")
    grps = lax.axis_size("grp")
    has_r, has_l = sub < subs - 1, sub > 0
    has_u, has_d = grp < grps - 1, grp > 0
    right, left = {"sub": sub + 1}, {"sub": sub - 1}
    up, down = {"grp": grp + 1}, {"grp": grp - 1}

    barrier = pltpu.get_barrier_semaphore()
    sides = ((has_r, right), (has_l, left), (has_u, up), (has_d, down))
    for has, device in sides:
        @pl.when(has)
        def _():
            pl.semaphore_signal(barrier, 1, device_id=device, device_id_type=MESH)

    loads = [
        pltpu.make_async_copy(src, dst, load_sem.at[i])
        for i, (src, dst) in enumerate(
            ((rows_h, rows), (res_h.at[0], res), (bas_h.at[0], bas), (cinv_h.at[0], cinv), (blk_h.at[0], blk),
             (links_h, links), (inv_h.at[0], inv), (mat_h.at[0], mat), (cols_h, cols))
        )
    ]
    for copy in loads:
        copy.start()

    def lend_copy(d, c):
        return pltpu.make_async_remote_copy(
            src_ref=lsend.at[d, c], dst_ref=lrecv.at[d, c], send_sem=ls_sem.at[d, c],
            recv_sem=lr_sem.at[d, c], device_id=(right, left)[d], device_id_type=MESH)

    def back_copy(d, c):
        return pltpu.make_async_remote_copy(
            src_ref=rsend.at[d, c], dst_ref=rrecv.at[d, c], send_sem=rs_sem.at[d, c],
            recv_sem=rr_sem.at[d, c], device_id=(right, left)[d], device_id_type=MESH)

    def level_copy(step, d):
        at = (1 + d) * COARSE
        return pltpu.make_async_remote_copy(
            src_ref=csend.at[step], dst_ref=xq.at[step, :, at : at + COARSE],
            send_sem=cs_sem.at[step, d], recv_sem=cr_sem.at[step, d],
            device_id=(up, down)[d], device_id_type=MESH)

    goes = (has_r, has_l)
    comes = (has_l, has_r)
    climbs = (has_u, has_d)
    falls = (has_d, has_u)

    for d in range(2):
        @pl.when(jnp.logical_not(comes[d]))
        def _():
            lrecv[d] = jnp.zeros(lrecv.shape[1:], BF)
            rrecv[d] = jnp.zeros(rrecv.shape[1:], BF)

        @pl.when(jnp.logical_not(falls[d]))
        def _():
            for step in range(2):
                at = (1 + d) * COARSE
                xq[step, :, at : at + COARSE] = jnp.zeros((2, COARSE, RHS), BF)

    loads[0].wait()
    loads[1].wait()
    for c in range(CHUNKS):
        for o in range(LEND):
            lsend[0, c, o] = res[1, rows[0, 1, 1, o], :, cols_of(c)]
            lsend[1, c, o] = res[0, rows[0, 0, 0, o], :, cols_of(c)]
    count = sum(has.astype(jnp.int32) for has, _ in sides)
    pl.semaphore_wait(barrier, count)
    for c in range(CHUNKS):
        for d in range(2):
            @pl.when(goes[d])
            def _():
                lend_copy(d, c).start()

    loads[2].wait()
    loads[3].wait()
    for s in range(2):
        hi, lo = split(cinv[s])
        ia[s, :COARSE] = hi
        ia[s, COARSE:] = lo
        basis = jnp.concatenate([bas[s, n] for n in range(OWN)], axis=1)
        rhs = mm(basis, res[s].reshape(OWN * TILE, RHS))
        rhi, rlo = split(rhs)
        both = mm(ia[s], rhi)
        level = both[:COARSE] + both[COARSE:] + mm(hi, rlo)
        lv0[s] = level
        lhi, llo = split(level)
        csend[0, s] = lhi
        xq[0, s, :COARSE] = lhi
        xq[0, s, 3 * COARSE :] = llo
    for d in range(2):
        @pl.when(climbs[d])
        def _():
            level_copy(0, d).start()

    loads[4].wait()
    loads[5].wait()
    for s in range(2):
        for n in range(OWN):
            bast[s, n * TILE : (n + 1) * TILE, :] = bas[s, n].T
        for j in range(3):
            q = jnp.dot(cinv[s], blk[s, j], precision=lax.Precision.HIGHEST, preferred_element_type=F32)
            if j:
                q = q * links[0, s, j - 1].astype(F32)
            hi, lo = split(q)
            at = j * COARSE
            qa[s, :COARSE, at : at + COARSE] = hi
            qa[s, COARSE:, at : at + COARSE] = lo
            if j == 0:
                qa[s, :COARSE, 3 * COARSE :] = hi
                qa[s, COARSE:, 3 * COARSE :] = jnp.zeros_like(lo)

    loads[6].wait()

    def first(s, e, b, c=None):
        y = mm(inv[s, e], b)
        where = slice(None) if c is None else cols_of(c)
        x0f[s, e, :, where] = y
        x0[s, e, :, where] = y.astype(BF)

    for s in range(2):
        for n in range(OWN):
            first(s, LEND + n, res[s, n])
    for o in range(LEND):
        first(0, LEND + OWN + o, res[1, rows[0, 1, 0, o]])
        first(1, o, res[0, rows[0, 0, 1, o]])

    loads[7].wait()
    loads[8].wait()
    for s in range(2):
        for e in range(EXT):
            tiles = jnp.concatenate([mat[s, e, k] for k in range(3)], axis=1)
            q = mm(inv[s, e], tiles).astype(BF)
            for k in range(3):
                mat[s, e, k] = q[:, k * TILE : (k + 1) * TILE]

    def swept(s, e, c, x):
        tiles = jnp.concatenate([mat[s, e, k] for k in range(3)], axis=1)
        picked = jnp.concatenate([x[s, cols[0, k, s, e], :, cols_of(c)] for k in range(3)], axis=0)
        y = x0f[s, e, :, cols_of(c)] + x[s, e, :, cols_of(c)].astype(F32) - mm(tiles, picked)
        return y.astype(BF)

    def level_step(step):
        for d in range(2):
            @pl.when(falls[d])
            def _():
                level_copy(step, d).wait_recv()
        for s in range(2):
            both = mm(qa[s], xq[step, s])
            old = lv0[s] if step == 0 else lv[s]
            level = old + lv0[s] - (both[:COARSE] + both[COARSE:])
            if step == 0:
                lv[s] = level
                lhi, llo = split(level)
                csend[1, s] = lhi
                xq[1, s, :COARSE] = lhi
                xq[1, s, 3 * COARSE :] = llo
            else:
                lev_b[s] = level.astype(BF)
        if step == 0:
            for d in range(2):
                @pl.when(climbs[d])
                def _():
                    level_copy(1, d).start()

    for c in range(CHUNKS):
        for d in range(2):
            @pl.when(comes[d])
            def _():
                lend_copy(d, c).wait_recv()
        for o in range(LEND):
            first(0, o, lrecv[0, c, o], c)
            first(1, LEND + OWN + o, lrecv[1, c, o], c)
        for s in range(2):
            for e in range(EXT):
                x1[s, e, :, cols_of(c)] = swept(s, e, c, x0)
        for o in range(LEND):
            rsend[0, c, o] = swept(1, LEND + OWN + o, c, x1)
            rsend[1, c, o] = swept(0, o, c, x1)
        for d in range(2):
            @pl.when(goes[d])
            def _():
                back_copy(d, c).start()
        if c == 0:
            level_step(0)
    for c in range(CHUNKS):
        for e in range(LEND, EXT):
            x2[0, e, :, cols_of(c)] = swept(0, e, c, x1)
        for e in range(LEND + OWN):
            x2[1, e, :, cols_of(c)] = swept(1, e, c, x1)
    level_step(1)

    for s in range(2):
        spread = mm(bast[s], lev_b[s])
        for n in range(OWN):
            y = x2[s, LEND + n].astype(F32) + spread[n * TILE : (n + 1) * TILE]
            for o in range(LEND):
                mark = (rows[0, s, 1 - s, o] == n).astype(F32)
                y = y + mark * x2[1 - s, (0 if s == 0 else LEND + OWN) + o].astype(F32)
            pre[s, n] = y

    for c in range(CHUNKS):
        for d in range(2):
            @pl.when(comes[d])
            def _():
                back_copy(d, c).wait_recv()
        for s in range(2):
            for n in range(OWN):
                y = pre[s, n, :, cols_of(c)]
                for o in range(LEND):
                    mark = (rows[0, s, s, o] == n).astype(F32)
                    y = y + mark * rrecv[s, c, o].astype(F32)
                out[0, s, n, :, cols_of(c)] = y.astype(BF)

    for d in range(2):
        @pl.when(goes[d])
        def _():
            for c in range(CHUNKS):
                lend_copy(d, c).wait_send()
                back_copy(d, c).wait_send()

        @pl.when(climbs[d])
        def _():
            for step in range(2):
                level_copy(step, d).wait_send()


def body(*args):
    residual, mat, inv, cols, rows, basis, blocks, coarse_inverse, links = args
    args = (residual, mat, inv, jnp.transpose(cols, (0, 3, 1, 2)), rows,
            jnp.transpose(basis, (0, 1, 3, 2, 4)), blocks, coarse_inverse, links)
    vm, sm, dma = pltpu.VMEM, pltpu.SMEM, pltpu.SemaphoreType.DMA
    ext = (2, EXT, TILE, RHS)
    moved = (2, CHUNKS, LEND, TILE, WIDTH)
    return pl.pallas_call(
        kernel,
        out_shape=pltpu.VMEM(residual.shape, BF),
        in_specs=[pl.BlockSpec(memory_space=pl.ANY)] * 9,
        out_specs=pl.BlockSpec(memory_space=pltpu.VMEM),
        scratch_shapes=[
            sm((1, 3, 2, EXT), jnp.int32), sm((1, 2, 2, LEND), jnp.int32), sm((1, 2, 2), jnp.int32),
            vm((2, OWN, TILE, RHS), BF), vm((2, EXT, 3, TILE, TILE), BF), vm((2, EXT, TILE, TILE), BF),
            vm((2, OWN, COARSE, TILE), BF), vm((2, 3, COARSE, COARSE), F32), vm((2, COARSE, COARSE), F32),
            vm((2, OWN * TILE, COARSE), BF),
            vm(ext, F32), vm(ext, BF), vm(ext, BF), vm(ext, BF), vm((2, OWN, TILE, RHS), F32),
            vm(moved, BF), vm(moved, BF), vm(moved, BF), vm(moved, BF),
            vm((2, 2 * COARSE, 4 * COARSE), BF), vm((2, 2 * COARSE, COARSE), BF),
            vm((2, 2, 4 * COARSE, RHS), BF), vm((2, COARSE, RHS), F32), vm((2, COARSE, RHS), F32),
            vm((2, 2, COARSE, RHS), BF), vm((2, COARSE, RHS), BF),
            dma((9,)), dma((2, CHUNKS)), dma((2, CHUNKS)), dma((2, CHUNKS)), dma((2, CHUNKS)),
            dma((2, 2)), dma((2, 2)),
        ],
        compiler_params=pltpu.CompilerParams(
            collective_id=0, has_side_effects=True, vmem_limit_bytes=58 * 1024 * 1024
        ),
        cost_estimate=pl.CostEstimate(flops=2_000_000_000, bytes_accessed=5_000_000, transcendentals=0),
        name="schwarz",
    )(*args)


def solution(mesh):
    in_specs = (
        P("grp", "sub", None, None, None),
        P("grp", "sub", None, None, None, None),
        P("grp", "sub", None, None, None),
        P("grp", "sub", None, None),
        P("grp", "sub", None, None),
        P("grp", "sub", None, None, None),
        P("grp", "sub", None, None, None),
        P("grp", "sub", None, None),
        P("grp", "sub", None),
    )
    out_specs = P("grp", "sub", None, None, None)
    return jax.shard_map(body, mesh=mesh, in_specs=in_specs, out_specs=out_specs, check_vma=False)
```

```python
import jax
import jax.numpy as jnp
from jax import lax
from jax.experimental import pallas as pl
from jax.experimental.pallas import tpu as pltpu
from jax.sharding import PartitionSpec as P

MESH = pl.DeviceIdType.MESH
BF = jnp.bfloat16
F32 = jnp.float32
OWN, EXT, LEND, TILE, RHS, COARSE = 6, 12, 3, 128, 256, 64
WIDTH = 128
CHUNKS = RHS // WIDTH


def mm(a, b):
    return jnp.dot(a, b, preferred_element_type=F32)


def split(a):
    hi = a.astype(BF)
    return hi, (a - hi.astype(F32)).astype(BF)


def cols_of(c):
    return slice(c * WIDTH, (c + 1) * WIDTH)


def kernel(
    res_h, mat_h, inv_h, cols_h, rows_h, bas_h, blk_h, cinv_h, links_h,
    out,
    cols, rows, links, res, mat, inv, bas, blk, cinv, bast,
    x0f, x0, x1, x2, pre,
    lsend, lrecv, rsend, rrecv,
    qa, ia, xq, lv0, lv, csend, lev_b,
    load_sem, ls_sem, lr_sem, rs_sem, rr_sem, cs_sem, cr_sem,
):
    sub = lax.axis_index("sub")
    grp = lax.axis_index("grp")
    subs = lax.axis_size("sub")
    grps = lax.axis_size("grp")
    has_r, has_l = sub < subs - 1, sub > 0
    has_u, has_d = grp < grps - 1, grp > 0
    right, left = {"sub": sub + 1}, {"sub": sub - 1}
    up, down = {"grp": grp + 1}, {"grp": grp - 1}

    barrier = pltpu.get_barrier_semaphore()
    sides = ((has_r, right), (has_l, left), (has_u, up), (has_d, down))
    for has, device in sides:
        @pl.when(has)
        def _():
            pl.semaphore_signal(barrier, 1, device_id=device, device_id_type=MESH)

    loads = [
        pltpu.make_async_copy(src, dst, load_sem.at[i])
        for i, (src, dst) in enumerate(
            ((rows_h, rows), (res_h.at[0], res), (bas_h.at[0], bas), (cinv_h.at[0], cinv), (blk_h.at[0], blk),
             (links_h, links), (inv_h.at[0], inv), (mat_h.at[0], mat), (cols_h, cols))
        )
    ]
    for copy in loads[:2]:
        copy.start()

    def lend_copy(d, c):
        return pltpu.make_async_remote_copy(
            src_ref=lsend.at[d, c], dst_ref=lrecv.at[d, c], send_sem=ls_sem.at[d, c],
            recv_sem=lr_sem.at[d, c], device_id={"sub": sub + 1 - 2 * d}, device_id_type=MESH)

    def back_copy(d, c):
        return pltpu.make_async_remote_copy(
            src_ref=rsend.at[d, c], dst_ref=rrecv.at[d, c], send_sem=rs_sem.at[d, c],
            recv_sem=rr_sem.at[d, c], device_id={"sub": sub + 1 - 2 * d}, device_id_type=MESH)

    def level_copy(step, d):
        at = (1 + d) * COARSE
        return pltpu.make_async_remote_copy(
            src_ref=csend.at[step], dst_ref=xq.at[step, :, at : at + COARSE],
            send_sem=cs_sem.at[step, d], recv_sem=cr_sem.at[step, d],
            device_id=(up, down)[d], device_id_type=MESH)

    goes = (has_r, has_l)
    comes = (has_l, has_r)
    climbs = (has_u, has_d)
    falls = (has_d, has_u)

    for d in range(2):
        @pl.when(jnp.logical_not(comes[d]))
        def _():
            lrecv[d] = jnp.zeros(lrecv.shape[1:], BF)
            rrecv[d] = jnp.zeros(rrecv.shape[1:], BF)

        @pl.when(jnp.logical_not(falls[d]))
        def _():
            for step in range(2):
                at = (1 + d) * COARSE
                xq[step, :, at : at + COARSE] = jnp.zeros((2, COARSE, RHS), BF)

    loads[0].wait()
    loads[1].wait()
    for copy in loads[2:]:
        copy.start()
    for c in range(CHUNKS):
        for o in range(LEND):
            lsend[0, c, o] = res[1, rows[0, 1, 1, o], :, cols_of(c)]
            lsend[1, c, o] = res[0, rows[0, 0, 0, o], :, cols_of(c)]
    loads[2].wait()
    loads[3].wait()
    for s in range(2):
        hi, lo = split(cinv[s])
        ia[s, :COARSE] = hi
        ia[s, COARSE:] = lo
        basis = jnp.concatenate([bas[s, n] for n in range(OWN)], axis=1)
        rhs = mm(basis, res[s].reshape(OWN * TILE, RHS))
        rhi, rlo = split(rhs)
        both = mm(ia[s], rhi)
        level = both[:COARSE] + both[COARSE:] + mm(hi, rlo)
        lv0[s] = level
        lhi, llo = split(level)
        csend[0, s] = lhi
        xq[0, s, :COARSE] = lhi
        xq[0, s, 3 * COARSE :] = llo
    count = sum(has.astype(jnp.int32) for has, _ in sides)
    pl.semaphore_wait(barrier, count)
    for c in range(CHUNKS):
        for d in range(2):
            @pl.when(goes[d])
            def _():
                lend_copy(d, c).start()

    for d in range(2):
        @pl.when(climbs[d])
        def _():
            level_copy(0, d).start()

    loads[4].wait()
    loads[5].wait()
    for s in range(2):
        for n in range(OWN):
            bast[s, n * TILE : (n + 1) * TILE, :] = bas[s, n].T
        for j in range(3):
            q = jnp.dot(cinv[s], blk[s, j], precision=lax.Precision.HIGHEST, preferred_element_type=F32)
            if j:
                q = q * links[0, s, j - 1].astype(F32)
            hi, lo = split(q)
            at = j * COARSE
            qa[s, :COARSE, at : at + COARSE] = hi
            qa[s, COARSE:, at : at + COARSE] = lo
            if j == 0:
                qa[s, :COARSE, 3 * COARSE :] = hi
                qa[s, COARSE:, 3 * COARSE :] = jnp.zeros_like(lo)

    loads[6].wait()

    def first(s, e, b):
        y = mm(inv[s, e], b)
        for c in range(CHUNKS):
            x0f[c, s, e] = y[:, cols_of(c)]
            x0[c, s, e] = y[:, cols_of(c)].astype(BF)

    @pl.loop(0, 2)
    def _(s):
        for n in range(OWN):
            first(s, LEND + n, res[s, n])
        for o in range(LEND):
            first(s, (1 - s) * (LEND + OWN) + o, res[1 - s, rows[0, 1 - s, s, o]])

    loads[7].wait()
    loads[8].wait()

    @pl.loop(0, 2)
    def _(s):
        for e in range(EXT):
            tiles = jnp.concatenate([mat[s, e, k] for k in range(3)], axis=1)
            q = mm(inv[s, e], tiles).astype(BF)
            for k in range(3):
                mat[s, e, k] = q[:, k * TILE : (k + 1) * TILE]

    def swept(s, e, c, x):
        tiles = jnp.concatenate([mat[s, e, k] for k in range(3)], axis=1)
        picked = jnp.concatenate([x[c, s, cols[0, k, s, e]] for k in range(3)], axis=0)
        y = x0f[c, s, e] + x[c, s, e].astype(F32) - mm(tiles, picked)
        return y.astype(BF)

    def level_step(step):
        for d in range(2):
            @pl.when(falls[d])
            def _():
                level_copy(step, d).wait_recv()
        for s in range(2):
            both = mm(qa[s], xq[step, s])
            old = lv0[s] if step == 0 else lv[s]
            level = old + lv0[s] - (both[:COARSE] + both[COARSE:])
            if step == 0:
                lv[s] = level
                lhi, llo = split(level)
                csend[1, s] = lhi
                xq[1, s, :COARSE] = lhi
                xq[1, s, 3 * COARSE :] = llo
            else:
                lev_b[s] = level.astype(BF)
        if step == 0:
            for d in range(2):
                @pl.when(climbs[d])
                def _():
                    level_copy(1, d).start()

    early = (sub % 4 == 0).astype(jnp.int32)

    def beside(s):
        return jnp.where(s == 0, has_l, has_r)

    def solve(s, c):
        @pl.when(beside(s))
        def _():
            lend_copy(s, c).wait_recv()
        edge = s * (LEND + OWN)
        for o in range(LEND):
            y = mm(inv[s, edge + o], lrecv[s, c, o])
            x0f[c, s, edge + o] = y
            x0[c, s, edge + o] = y.astype(BF)
        for e in range(EXT):
            x1[c, s, e] = swept(s, e, c, x0)
        for o in range(LEND):
            rsend[1 - s, c, o] = swept(s, edge + o, c, x1)

        @pl.when(beside(s))
        def _():
            back_copy(1 - s, c).start()

    def finish(s, c):
        kept = (1 - s) * LEND
        for e in range(LEND + OWN):
            x2[c, s, kept + e] = swept(s, kept + e, c, x1)

    pl.loop(0, CHUNKS)(lambda c: solve(early, c))
    pl.loop(0, CHUNKS)(lambda c: finish(early, c))
    level_step(0)
    pl.loop(0, CHUNKS)(lambda c: solve(1 - early, c))
    pl.loop(0, CHUNKS)(lambda c: finish(1 - early, c))
    level_step(1)

    @pl.loop(0, 2)
    def _(s):
        spread = mm(bast[s], lev_b[s])
        for c in range(CHUNKS):
            for n in range(OWN):
                y = x2[c, s, LEND + n].astype(F32) + spread[n * TILE : (n + 1) * TILE, cols_of(c)]
                for o in range(LEND):
                    mark = (rows[0, s, 1 - s, o] == n).astype(F32)
                    y = y + mark * x2[c, 1 - s, s * (LEND + OWN) + o].astype(F32)
                pre[c, s, n] = y

    for i in range(2):
        s = early if i == 0 else 1 - early
        for c in range(CHUNKS):
            @pl.when(beside(s))
            def _():
                back_copy(s, c).wait_recv()
            for n in range(OWN):
                y = pre[c, s, n]
                for o in range(LEND):
                    mark = (rows[0, s, s, o] == n).astype(F32)
                    y = y + mark * rrecv[s, c, o].astype(F32)
                out[0, s, n, :, cols_of(c)] = y.astype(BF)

    for d in range(2):
        @pl.when(goes[d])
        def _():
            for c in range(CHUNKS):
                lend_copy(d, c).wait_send()
                back_copy(d, c).wait_send()

        @pl.when(climbs[d])
        def _():
            for step in range(2):
                level_copy(step, d).wait_send()


def body(*args):
    residual, mat, inv, cols, rows, basis, blocks, coarse_inverse, links = args
    args = (residual, mat, inv, jnp.transpose(cols, (0, 3, 1, 2)), rows,
            jnp.transpose(basis, (0, 1, 3, 2, 4)), blocks, coarse_inverse, links)
    vm, sm, dma = pltpu.VMEM, pltpu.SMEM, pltpu.SemaphoreType.DMA
    ext = (CHUNKS, 2, EXT, TILE, WIDTH)
    moved = (2, CHUNKS, LEND, TILE, WIDTH)
    return pl.pallas_call(
        kernel,
        out_shape=pltpu.VMEM(residual.shape, BF),
        in_specs=[pl.BlockSpec(memory_space=pl.ANY)] * 9,
        out_specs=pl.BlockSpec(memory_space=pltpu.VMEM),
        scratch_shapes=[
            sm((1, 3, 2, EXT), jnp.int32), sm((1, 2, 2, LEND), jnp.int32), sm((1, 2, 2), jnp.int32),
            vm((2, OWN, TILE, RHS), BF), vm((2, EXT, 3, TILE, TILE), BF), vm((2, EXT, TILE, TILE), BF),
            vm((2, OWN, COARSE, TILE), BF), vm((2, 3, COARSE, COARSE), F32), vm((2, COARSE, COARSE), F32),
            vm((2, OWN * TILE, COARSE), BF),
            vm(ext, F32), vm(ext, BF), vm(ext, BF), vm(ext, BF), vm((CHUNKS, 2, OWN, TILE, WIDTH), F32),
            vm(moved, BF), vm(moved, BF), vm(moved, BF), vm(moved, BF),
            vm((2, 2 * COARSE, 4 * COARSE), BF), vm((2, 2 * COARSE, COARSE), BF),
            vm((2, 2, 4 * COARSE, RHS), BF), vm((2, COARSE, RHS), F32), vm((2, COARSE, RHS), F32),
            vm((2, 2, COARSE, RHS), BF), vm((2, COARSE, RHS), BF),
            dma((9,)), dma((2, CHUNKS)), dma((2, CHUNKS)), dma((2, CHUNKS)), dma((2, CHUNKS)),
            dma((2, 2)), dma((2, 2)),
        ],
        compiler_params=pltpu.CompilerParams(
            collective_id=0, has_side_effects=True, vmem_limit_bytes=58 * 1024 * 1024
        ),
        cost_estimate=pl.CostEstimate(flops=2_000_000_000, bytes_accessed=5_000_000, transcendentals=0),
        name="schwarz",
    )(*args)


def solution(mesh):
    in_specs = (
        P("grp", "sub", None, None, None),
        P("grp", "sub", None, None, None, None),
        P("grp", "sub", None, None, None),
        P("grp", "sub", None, None),
        P("grp", "sub", None, None),
        P("grp", "sub", None, None, None),
        P("grp", "sub", None, None, None),
        P("grp", "sub", None, None),
        P("grp", "sub", None),
    )
    out_specs = P("grp", "sub", None, None, None)
    return jax.shard_map(body, mesh=mesh, in_specs=in_specs, out_specs=out_specs, check_vma=False)
```
